256 devices in a mesh: blk: 32 (over y_hi, z, core), head: 8 (over x, y_lo).
Axes of the slice: x: 4, y: 4 (y_hi: 2, y_lo: 2; y = y_hi * 2 + y_lo), z: 8, core: 2. Of those that a mesh axis runs over, the one named last changes fastest.
Arguments:
- query_content: bfloat16 [32, 128, 64, 128], P('blk', None, 'head'), may hold values from -12 to 12
- query_rotary: bfloat16 [32, 64, 64, 128], P('blk', 'head'), may hold values from -48 to 48
- prompt_latent: bfloat16 [512, 4096], P(None, 'blk'), may hold values from -7 to 7
- prompt_rotary: bfloat16 [64, 4096], P(None, 'blk'), may hold values from -6 to 6
- reply_latent: bfloat16 [32, 512, 128], P('blk'), may hold values from -6 to 6
- reply_rotary: bfloat16 [32, 64, 128], P('blk'), may hold values from -6 to 6
- key_weight: bfloat16 [64, 128, 512], P('head'), may hold values from -0.25 to 0.25
- value_weight: bfloat16 [64, 512, 128], P('head'), may hold values from -1 to 1
- output_weight: bfloat16 [64, 128, 3584], P('head'), may hold values from -0.125 to 0.125
- lengths: int32 [32], P('blk'), may hold values from 32 to 128, as said below
- offsets: int32 [32], P('blk'), may hold values from 1024 to 4096, as said below
Outputs:
- layer_output: bfloat16 [128, 32, 3584], P('head', 'blk')
The draws below stay inside these ranges and needn't reach their ends.
Inputs may be any that keep to these rules, and one draw needn't show every extreme that they name: `lengths`: some reply has all 128 slots. `offsets`: some reply sees all 4096 positions.
All inputs are finite; a program needn't handle non-finite values.
Results may differ from the reference program's by a relative error of at most 0.02.
Values may be sent and summed in bfloat16 or wider, within the bound.
No kernel may reach another device: no remote copies, remote signals or barrier semaphores. Data moves between devices by JAX's collectives and lax.ppermute only.
A program may use at most 64 MiB of HBM per device.

```python
import jax
import jax.numpy as jnp
from jax import lax

HEADS = 64
CONTENT = 128
ROTARY = 64
LATENT = 512
VALUE_SIZE = 128
WIDTH = 3584
REPLY_LEN = 128
REPLIES = 32
PROMPT = 4096


def draw_prompt_rotary(key, part):
    key = jax.random.fold_in(key, 11)
    return jax.random.truncated_normal(key, -6.0, 6.0, (ROTARY, PROMPT), jnp.float32).astype(jnp.bfloat16)


def draw_query_rotary(key, part):
    key = jax.random.fold_in(key, 12)
    return jax.random.truncated_normal(key, -6.0, 6.0, (REPLIES, HEADS, ROTARY, REPLY_LEN), jnp.float32).astype(jnp.bfloat16)


def draw_prompt_latent(key, part):
    key = jax.random.fold_in(key, 13)
    return jax.random.truncated_normal(key, -6.0, 6.0, (LATENT, PROMPT), jnp.float32).astype(jnp.bfloat16)


def draw_lengths(key, part):
    key = jax.random.fold_in(key, 14)
    keys = jax.random.split(key, 2)
    drawn = jax.random.randint(keys[0], (REPLIES,), REPLY_LEN // 4, REPLY_LEN + 1)
    full = jax.random.randint(keys[1], (), 0, REPLIES)
    return jnp.where(jnp.arange(REPLIES) == full, REPLY_LEN, drawn).astype(jnp.int32)


def draw_offsets(key, part):
    key = jax.random.fold_in(key, 15)
    keys = jax.random.split(key, 2)
    drawn = jax.random.randint(keys[0], (REPLIES,), PROMPT // 4, PROMPT + 1)
    full = jax.random.randint(keys[1], (), 0, REPLIES)
    return jnp.where(jnp.arange(REPLIES) == full, PROMPT, drawn).astype(jnp.int32)


def steps_of(rng, dims, cuts, low, top_value):
    def one(axis_at, blocks):
        heights = jax.random.uniform(jax.random.fold_in(jax.random.fold_in(rng, 6), axis_at), (blocks,), jnp.float32, low / len(cuts), top_value / len(cuts))
        return jnp.repeat(jnp.exp(heights), dims[axis_at] // blocks).reshape((-1,) + (1,) * (len(dims) - axis_at - 1))

    loudness = one(*cuts[0])
    for cut in cuts[1:]:
        loudness = loudness * one(*cut)
    return loudness


def centred(rng, shape, width, most, pieces=(), kind=jnp.bfloat16):
    level = steps_of(rng, shape, pieces, -0.22, 0.18) if pieces else 1.0
    result = jax.random.normal(rng, shape, jnp.float32) * width * level
    return jnp.minimum(jnp.maximum(result, -most), most).astype(kind)


def setup_inputs(seed: int = 0) -> dict:
    key_of = jax.random.split(jax.random.key(seed), 12)
    query_content = centred(key_of[0], (REPLIES, REPLY_LEN, HEADS, CONTENT), 2.0, 12.0, ((0, 32), (2, 8)))
    query_rotary = draw_query_rotary(jax.random.fold_in(key_of[11], 71), 0)
    prompt_latent = draw_prompt_latent(jax.random.fold_in(key_of[11], 71), 0)
    prompt_rotary = draw_prompt_rotary(jax.random.fold_in(key_of[11], 71), 0)
    reply_latent = centred(key_of[4], (REPLIES, LATENT, REPLY_LEN), 1.0, 6.0, ((0, 32),))
    reply_rotary = centred(key_of[5], (REPLIES, ROTARY, REPLY_LEN), 1.0, 6.0, ((0, 32),))
    key_weight = centred(key_of[6], (HEADS, CONTENT, LATENT), LATENT ** -0.5, 0.25, ((0, 8),))
    value_weight = centred(key_of[7], (HEADS, LATENT, VALUE_SIZE), (LATENT // 16) ** -0.5, 1.0, ((0, 8),))
    output_weight = centred(key_of[8], (HEADS, VALUE_SIZE, WIDTH), (HEADS * VALUE_SIZE // 4) ** -0.5, 0.125, ((0, 8),))
    lengths = draw_lengths(jax.random.fold_in(key_of[11], 71), 0)
    offsets = draw_offsets(jax.random.fold_in(key_of[11], 71), 0)
    return {"query_content": query_content, "query_rotary": query_rotary, "prompt_latent": prompt_latent, "prompt_rotary": prompt_rotary, "reply_latent": reply_latent, "reply_rotary": reply_rotary, "key_weight": key_weight, "value_weight": value_weight, "output_weight": output_weight, "lengths": lengths, "offsets": offsets}


NEGATIVE = -1.0e30


def rounded(value):
    return lax.optimization_barrier(value.astype(jnp.bfloat16)).astype(jnp.float32)


def reference(query_content, query_rotary, prompt_latent, prompt_rotary, reply_latent, reply_rotary, key_weight, value_weight, output_weight, lengths, offsets):
    scale = (CONTENT + ROTARY) ** -0.5
    places = jnp.arange(PROMPT, dtype=jnp.int32)
    positions = jnp.arange(REPLY_LEN, dtype=jnp.int32)
    causal = positions[:, None] >= positions[None, :]
    latent_all = prompt_latent.astype(jnp.float32)
    rotary_all = prompt_rotary.astype(jnp.float32)
    key_full = key_weight.astype(jnp.float32)
    value_full = value_weight.astype(jnp.float32)
    output_full = output_weight.astype(jnp.float32)

    def one_reply(index):
        content = lax.dynamic_index_in_dim(query_content, index, 0, keepdims=False).astype(jnp.float32)
        rotary = lax.dynamic_index_in_dim(query_rotary, index, 0, keepdims=False).astype(jnp.float32)
        own_latent = lax.dynamic_index_in_dim(reply_latent, index, 0, keepdims=False).astype(jnp.float32)
        own_rotary = lax.dynamic_index_in_dim(reply_rotary, index, 0, keepdims=False).astype(jnp.float32)
        limit = lax.dynamic_index_in_dim(offsets, index, 0, keepdims=False)
        length = lax.dynamic_index_in_dim(lengths, index, 0, keepdims=False)
        query_latent = rounded(jnp.einsum("thn,hnc->htc", content, key_full))
        prompt_scores = scale * (jnp.einsum("htc,cn->htn", query_latent, latent_all) + jnp.einsum("het,en->htn", rotary, rotary_all))
        prompt_scores = jnp.where(places[None, None, :] < limit, prompt_scores, NEGATIVE)
        own_scores = scale * (jnp.einsum("htc,cn->htn", query_latent, own_latent) + jnp.einsum("het,en->htn", rotary, own_rotary))
        own_scores = jnp.where(causal[None], own_scores, NEGATIVE)
        peak = jnp.maximum(jnp.max(prompt_scores, axis=-1), jnp.max(own_scores, axis=-1))
        prompt_weights = jnp.exp(prompt_scores - peak[..., None])
        own_weights = jnp.exp(own_scores - peak[..., None])
        total = jnp.sum(prompt_weights, axis=-1) + jnp.sum(own_weights, axis=-1)
        summed = jnp.einsum("htn,cn->htc", rounded(prompt_weights), latent_all) + jnp.einsum("htn,cn->htc", rounded(own_weights), own_latent)
        latent_out = rounded(summed / total[..., None])
        values = rounded(jnp.einsum("htc,hcv->thv", latent_out, value_full))
        term = jnp.einsum("thv,hvd->td", values, output_full)
        live = positions < length
        return jnp.where(live[:, None], term, 0.0).astype(jnp.bfloat16)

    stacked = lax.map(one_reply, jnp.arange(REPLIES, dtype=jnp.int32))
    return jnp.transpose(stacked, (1, 0, 2))
```

```python
import functools
import itertools
import math

import jax
import jax.numpy as jnp
import numpy as np
from jax import lax
from jax.experimental import pallas as pl
from jax.experimental.pallas import tpu as pltpu
from jax.sharding import PartitionSpec as P

NEGATIVE = -1e30
EMPTY = -1e29
AXES = ("blk", "head")
SIZES = (2, 8, 2, 4, 2)
KEYS = 128
DEPTH = 576
PADDED = 640


def linear(place):
    index = 0
    for value, size in zip(place, SIZES):
        index = index * size + value % size
    return index


PLACES = list(itertools.product(*map(range, SIZES)))


def pairs_from(source):
    return [(linear(source(*place)), linear(place)) for place in PLACES]


def side(core):
    return 1 - 2 * core


def fetch(far):
    def source(yh, z, core, x, yl):
        wide = (x + 2 * yl) % 4 // 2
        distance = ((1, 3), (2, 4 if core == 0 else 0))[wide][far]
        z = z - distance * side(core)
        if x % 2:
            return 1 - yh, z, core, x, 1 - yl
        return yh, z, core, x, yl

    return source


def other_core(yh, z, core, x, yl):
    return yh, z, 1 - core, x, yl


def from_x(step):
    return lambda yh, z, core, x, yl: (yh, z, core, x - step, yl)


def from_y(yh, z, core, x, yl):
    return yh, z, core, x, 1 - yl


def take(held, source):
    array, numbers = held
    pairs = pairs_from(source)
    moved = np.empty_like(numbers)
    for start, end in pairs:
        moved[end] = numbers[start]
    return lax.ppermute(array, AXES, pairs), moved


def joined(*held):
    return jnp.concatenate([h[0] for h in held], 0), np.concatenate([h[1] for h in held], 1)


def attend(query, keys, numbers, offsets, own, state, value_weight, sub, subs):
    rows = query.shape[0]
    half = rows // 2
    counts = [k.shape[0] for k in keys]
    shards = sum(counts)
    total_keys = (shards + (own is not None)) * KEYS
    block = sub * subs
    scale = (128 + 64) ** -0.5 * math.log2(math.e)
    first, last = state is None, value_weight is not None

    def kernel(numbers_ref, offsets_ref, query_ref, *refs):
        refs = list(refs)
        key_refs = [refs.pop(0) for _ in keys]
        own_ref = refs.pop(0) if first else None
        stats_in, sum_in = (None, None) if first else (refs.pop(0), refs.pop(0))
        weight_ref = refs.pop(0) if last else None
        if last:
            values_out = refs.pop(0)
        else:
            stats_out, sum_out = refs.pop(0), refs.pop(0)
        table = refs.pop(0)
        step = pl.program_id(0)

        @pl.when(step == 0)
        def _():
            at = 0
            row = lax.broadcasted_iota(jnp.int32, (16, KEYS), 0)
            lane = lax.broadcasted_iota(jnp.int32, (16, KEYS), 1)
            limit = jnp.where(row == 0, offsets_ref[0], offsets_ref[1])
            for ref, count in zip(key_refs, counts):
                for i in range(count):
                    columns = slice(at * KEYS, (at + 1) * KEYS)
                    table[0:DEPTH, columns] = ref[i]
                    hidden = (row < 2) & (numbers_ref[at] * KEYS + lane >= limit)
                    table[DEPTH : DEPTH + 16, columns] = jnp.where(hidden, NEGATIVE, 0.0).astype(jnp.bfloat16)
                    at += 1
            if first:
                columns = slice(at * KEYS, (at + 1) * KEYS)
                table[0:DEPTH, columns] = own_ref[...]
                table[DEPTH : DEPTH + 16, columns] = jnp.where(row == 1, NEGATIVE, 0.0).astype(jnp.bfloat16)
            table[DEPTH + 16 : PADDED, :] = jnp.zeros((PADDED - DEPTH - 16, total_keys), jnp.bfloat16)

        def scores(i):
            found = jnp.dot(
                query_ref[i * sub : (i + 1) * sub, :], table[...], preferred_element_type=jnp.float32
            )
            if first:
                slot = lax.broadcasted_iota(jnp.int32, (sub, KEYS), 0) % KEYS
                key = lax.broadcasted_iota(jnp.int32, (sub, KEYS), 1)
                tail = jnp.where(key <= slot, found[:, shards * KEYS :], NEGATIVE)
                found = jnp.concatenate([found[:, : shards * KEYS], tail], axis=1)
            return found

        def finish(i, found):
            part = slice(i * sub, (i + 1) * sub)
            peak = jnp.max(found, axis=1, keepdims=True)
            if first:
                peak = jnp.maximum(peak, EMPTY)
            else:
                old_peak = stats_in[part, 0:1]
                peak = jnp.maximum(peak, old_peak)
                factor = jnp.exp2((old_peak - peak) * scale)
            weights = jnp.exp2(found * scale - peak * scale)
            total = jnp.sum(weights, axis=1, keepdims=True)
            summed = lax.dot_general(
                weights.astype(jnp.bfloat16),
                table[0:512, :],
                (((1,), (1,)), ((), ())),
                preferred_element_type=jnp.float32,
            )
            if not first:
                total = total + stats_in[part, 1:2] * factor
                summed = summed + sum_in[part, :] * factor
            if not last:
                lane = lax.broadcasted_iota(jnp.int32, (sub, KEYS), 1)
                stats_out[part, :] = jnp.where(lane == 0, peak, total)
                sum_out[part, :] = summed
                return
            seen = total > 0.0
            latent = (summed / jnp.where(seen, total, 1.0)).astype(jnp.bfloat16)
            level = jnp.where(seen, peak * scale + jnp.log2(jnp.where(seen, total, 1.0)), NEGATIVE)
            high = level.astype(jnp.bfloat16).astype(jnp.float32)
            middle = (level - high).astype(jnp.bfloat16).astype(jnp.float32)
            low = level - high - middle
            lane = lax.broadcasted_iota(jnp.int32, (sub, KEYS), 1)
            parts = jnp.where(lane == 0, high, jnp.where(lane == 1, middle, low))
            values_out[part, KEYS:] = parts.astype(jnp.bfloat16)
            for j in range(sub // KEYS):
                head = lax.rem(step * (block // KEYS) + i * (sub // KEYS) + j, half // KEYS)
                values_out[i * sub + j * KEYS : i * sub + (j + 1) * KEYS, :KEYS] = jnp.dot(
                    latent[j * KEYS : (j + 1) * KEYS, :],
                    weight_ref[head],
                    preferred_element_type=jnp.float32,
                ).astype(jnp.bfloat16)

        found = scores(0)
        for i in range(subs):
            following = scores(i + 1) if i + 1 < subs else None
            finish(i, found)
            found = following

    def tall(width):
        return pl.BlockSpec((block, width), lambda i, *_: (i, 0))

    def whole(array):
        return pl.BlockSpec(array.shape, lambda i, *_: (0,) * array.ndim)

    operands, specs = [query, *keys], [tall(PADDED), *map(whole, keys)]
    if first:
        operands.append(own)
        specs.append(whole(own))
    else:
        operands += state
        specs += [tall(KEYS), tall(512)]
    if last:
        operands.append(value_weight)
        specs.append(whole(value_weight))
        shapes = [jax.ShapeDtypeStruct((rows, 2 * KEYS), jnp.bfloat16)]
        outs = [tall(2 * KEYS)]
    else:
        shapes = [jax.ShapeDtypeStruct((rows, KEYS), jnp.float32), jax.ShapeDtypeStruct((rows, 512), jnp.float32)]
        outs = [tall(KEYS), tall(512)]
    return pl.pallas_call(
        kernel,
        grid_spec=pltpu.PrefetchScalarGridSpec(
            num_scalar_prefetch=2,
            grid=(rows // block,),
            in_specs=specs,
            out_specs=outs,
            scratch_shapes=[pltpu.VMEM((PADDED, total_keys), jnp.bfloat16)],
        ),
        out_shape=shapes,
        compiler_params=pltpu.CompilerParams(vmem_limit_bytes=48 * 2**20),
        cost_estimate=pl.CostEstimate(
            flops=2 * rows * total_keys * (PADDED + 512), bytes_accessed=8 << 20, transcendentals=rows * total_keys
        ),
    )(numbers, offsets, *operands)


def project(mine, theirs, output_weight, length):
    rows = mine.shape[0]
    heads = rows // KEYS
    width = output_weight.shape[-1]
    tile = 512

    def kernel(length_ref, mine_ref, theirs_ref, weight_ref, out_ref, values):
        @pl.when(pl.program_id(0) == 0)
        def _():
            def level(ref, part):
                found = ref[part, KEYS:].astype(jnp.float32)
                return found[:, 0:1] + (found[:, 1:2] + found[:, 2:3])

            for head in range(heads):
                part = slice(head * KEYS, (head + 1) * KEYS)
                a, b = level(mine_ref, part), level(theirs_ref, part)
                top = jnp.maximum(a, b)
                a, b = jnp.exp2(a - top), jnp.exp2(b - top)
                both = mine_ref[part, :KEYS].astype(jnp.float32) * a + theirs_ref[part, :KEYS].astype(jnp.float32) * b
                slot = lax.broadcasted_iota(jnp.int32, (KEYS, KEYS), 0)
                both = jnp.where(slot < length_ref[0], both / (a + b), 0.0)
                values[:, part] = both.astype(jnp.bfloat16)

        out_ref[...] = jnp.dot(values[...], weight_ref[...], preferred_element_type=jnp.float32).astype(jnp.bfloat16)

    return pl.pallas_call(
        kernel,
        grid_spec=pltpu.PrefetchScalarGridSpec(
            num_scalar_prefetch=1,
            grid=(width // tile,),
            in_specs=[
                pl.BlockSpec(mine.shape, lambda i, *_: (0, 0)),
                pl.BlockSpec(theirs.shape, lambda i, *_: (0, 0)),
                pl.BlockSpec((rows, tile), lambda i, *_: (0, i)),
            ],
            out_specs=pl.BlockSpec((KEYS, tile), lambda i, *_: (0, i)),
            scratch_shapes=[pltpu.VMEM((KEYS, rows), jnp.bfloat16)],
        ),
        out_shape=jax.ShapeDtypeStruct((KEYS, width), jnp.bfloat16),
        compiler_params=pltpu.CompilerParams(vmem_limit_bytes=32 * 2**20),
        cost_estimate=pl.CostEstimate(flops=2 * KEYS * rows * width, bytes_accessed=2 * rows * width, transcendentals=0),
    )(length, mine, theirs, output_weight)


def body(
    query_content,
    query_rotary,
    prompt_latent,
    prompt_rotary,
    reply_latent,
    reply_rotary,
    key_weight,
    value_weight,
    output_weight,
    lengths,
    offsets,
):
    device = lax.axis_index("blk") * lax.axis_size("head") + lax.axis_index("head")
    numbers = np.array([[linear(place) // 8] for place in PLACES], np.int32)
    mine = (jnp.concatenate([prompt_latent, prompt_rotary], 0)[None], numbers)
    chip = joined(mine, take(mine, other_core))
    near, far = take(chip, fetch(0)), take(chip, fetch(1))
    groups = [[near, far]]
    groups.append([take(h, s) for h in (near, far) for s in (from_x(1), from_x(-1), from_y)])

    heads, slots = key_weight.shape[0], query_content.shape[1]
    query_latent = jnp.einsum("thn,hnc->htc", query_content[0], key_weight, preferred_element_type=jnp.float32)
    query = jnp.concatenate([query_latent.astype(jnp.bfloat16), jnp.swapaxes(query_rotary[0], 1, 2)], -1)
    query = query.reshape(heads * slots, DEPTH)
    partner = pairs_from(other_core)
    query_theirs = lax.ppermute(query, AXES, partner)
    lane = jnp.arange(PADDED - DEPTH)
    marks = [jnp.broadcast_to((lane == i).astype(jnp.bfloat16), (heads * slots, PADDED - DEPTH)) for i in (0, 1)]
    query = jnp.concatenate(
        [jnp.concatenate([query, marks[0]], 1), jnp.concatenate([query_theirs, marks[1]], 1)], 0
    )
    limits = jnp.concatenate([offsets, lax.ppermute(offsets, AXES, partner)])
    own = jnp.concatenate([reply_latent[0], reply_rotary[0]], 0)

    state = None
    for at, group in enumerate(groups):
        table = np.concatenate([h[1] for h in group], 1)
        here = lax.dynamic_index_in_dim(jnp.asarray(table), device, 0, keepdims=False)
        weight = value_weight if at + 1 == len(groups) else None
        state = attend(query, [h[0] for h in group], here, limits, own if at == 0 else None, state, weight, 256, 2)
    (values,) = state
    rows = heads * slots
    theirs = lax.ppermute(values[rows:], AXES, partner)
    term = project(values[:rows], theirs, output_weight.reshape(rows, -1), lengths)
    parts = lax.all_to_all(term, "head", 0, 0, tiled=True)
    parts = parts.reshape(8, slots // 8, -1).astype(jnp.float32)
    return jnp.sum(parts, 0).astype(jnp.bfloat16)[:, None, :]


def solution(mesh):
    placed = (
        P("blk", None, "head", None),
        P("blk", "head", None, None),
        P(None, "blk"),
        P(None, "blk"),
        P("blk", None, None),
        P("blk", None, None),
        P("head", None, None),
        P("head", None, None),
        P("head", None, None),
        P("blk"),
        P("blk"),
    )
    return jax.shard_map(
        body, mesh=mesh, in_specs=placed, out_specs=P("head", "blk", None), check_vma=False
    )
```

```python
import functools
import itertools
import math

import jax
import jax.numpy as jnp
from jax import lax
from jax.experimental import pallas as pl
from jax.experimental.pallas import tpu as pltpu
from jax.sharding import PartitionSpec as P

NEGATIVE = -1e30
EMPTY = -1e29
AXES = ("blk", "head")
SIZES = (2, 8, 2, 4, 2)
KEYS = 128
DEPTH = 576
PADDED = 640


def linear(place):
    index = 0
    for value, size in zip(place, SIZES):
        index = index * size + value % size
    return index


PLACES = list(itertools.product(*map(range, SIZES)))


def pairs_from(source):
    return [(linear(source(*place)), linear(place)) for place in PLACES]


def side(core):
    return 1 - 2 * core


def fetch(far):
    def source(yh, z, core, x, yl):
        wide = (x + 2 * yl) % 4 // 2
        distance = (3 + wide * (1 - 4 * core)) if far else 1 + wide
        odd = x % 2
        return (yh + odd) % 2, (z + 8 - distance * side(core)) % 8, core, x, (yl + odd) % 2

    return source


def other_core(yh, z, core, x, yl):
    return yh, z, 1 - core, x, yl


def from_x(step):
    return lambda yh, z, core, x, yl: (yh, z, core, (x + 4 - step) % 4, yl)


def from_y(yh, z, core, x, yl):
    return yh, z, core, x, 1 - yl


def start_of(place):
    yh, z, core, _, _ = place
    return [(yh * 8 + z) * 2 + core]


class Shards:
    def __init__(self, array, numbers):
        self.array, self.numbers, self.count = array, numbers, array.shape[0]

    def taken(self, source):
        numbers = self.numbers
        return Shards(lax.ppermute(self.array, AXES, pairs_from(source)), lambda *place: numbers(*source(*place)))

    def joined(self, other):
        a, b = self.numbers, other.numbers
        return Shards(jnp.concatenate([self.array, other.array], 0), lambda *place: a(*place) + b(*place))


def own_place():
    blk, head = lax.axis_index("blk"), lax.axis_index("head")
    return blk // 16, blk // 2 % 8, blk % 2, head // 2, head % 2


def spread():
    return (lax.broadcasted_iota(jnp.int32, (KEYS, KEYS), 0) < 3).astype(jnp.float32).astype(jnp.bfloat16)


def level_of(parts):
    return jnp.dot(parts, spread(), preferred_element_type=jnp.float32)


def attend(queries, group, limits, own, value_weight):
    heads = value_weight.shape[0]
    rows = heads * KEYS
    shards = sum(g.count for g in group)
    first = int(own is not None)
    chunk = 4
    slots = 64
    sub = heads * slots
    scale = (128 + 64) ** -0.5 * math.log2(math.e)
    operands = [*limits, *queries, value_weight, *(g.array for g in group), *(own or ())]

    def kernel(*refs):
        refs = list(refs)
        limit_refs = [refs.pop(0) for _ in range(2)]
        query_refs = [refs.pop(0) for _ in queries]
        weight_ref = refs.pop(0)
        group_refs = [refs.pop(0) for _ in group]
        own_refs = [refs.pop(0) for _ in range(2)] if first else []
        out_refs = [refs.pop(0) for _ in range(2)]
        if first:
            query, table, weight, latents, levels, content, wide, rotary, absorbed, sems = refs
        else:
            table, weight, latents, levels, query, sems = refs
        copies = []

        def copy(start, end):
            made = pltpu.make_async_copy(start, end, sems.at[len(copies)])
            made.start()
            copies.append(made)

        place = own_place()
        numbers = [n for g in group for n in g.numbers(*place)]
        ranks = [sum((other < n).astype(jnp.int32) for other in numbers if other is not n) for n in numbers]
        if first:
            for ref, end in zip(query_refs, (content.at[0], content.at[1], rotary.at[0], rotary.at[1], absorbed)):
                copy(ref, end)
        else:
            copy(query_refs[0], query)
        for i, rank in enumerate(ranks):
            copy(group_refs[i // 2].at[i % 2], table.at[first + rank, pl.ds(0, DEPTH), :])
        if first:
            copy(own_refs[0], table.at[0, pl.ds(0, 512), :])
            copy(own_refs[1], table.at[0, pl.ds(512, 64), :])
        copy(weight_ref, weight)

        row = lax.broadcasted_iota(jnp.int32, (16, KEYS), 0)
        lane = lax.broadcasted_iota(jnp.int32, (16, KEYS), 1)
        limit = jnp.where(row == 0, limit_refs[0][0], limit_refs[1][0])
        hide = [(0, row == 1)] if first else []
        hide += [(first + rank, (row < 2) & (n * KEYS + lane >= limit)) for n, rank in zip(numbers, ranks)]
        for at, hidden in hide:
            table[at, DEPTH : DEPTH + 16, :] = jnp.where(hidden, NEGATIVE, 0.0).astype(jnp.bfloat16)
            table[at, DEPTH + 16 : PADDED, :] = jnp.zeros((PADDED - DEPTH - 16, KEYS), jnp.bfloat16)
        for made in copies[:-1]:
            made.wait()
        if first:
            lanes = lax.broadcasted_iota(jnp.int32, (KEYS, PADDED - DEPTH), 1)
            for slot in range(2):
                wide[...] = content[slot].astype(jnp.float32)
                for head in range(heads):
                    part = slice(head * KEYS, (head + 1) * KEYS)
                    asked = wide[pl.ds(head, KEYS, stride=heads), :].astype(jnp.bfloat16)
                    latent = jnp.dot(asked, absorbed[head], preferred_element_type=jnp.float32)
                    query[slot, part, 0:512] = latent.astype(jnp.bfloat16)
                    rest = [rotary[slot, head].astype(jnp.float32).T, (lanes == slot).astype(jnp.float32)]
                    query[slot, part, 512:PADDED] = jnp.concatenate(rest, 1).astype(jnp.bfloat16)

        def keys(begin, count, depth):
            return jnp.concatenate([table[at, :depth, :] for at in range(begin, begin + count)], 1)

        def work(slot, blocks, chunks):
            spans = [(0, 1)] * first + [(first + i * chunk, chunk) for i in range(chunks)]
            key = lax.broadcasted_iota(jnp.int32, (sub, KEYS), 1)
            time = lax.broadcasted_iota(jnp.int32, (sub, KEYS), 0) % slots
            held = None
            for block in range(blocks + 1):
                found, top = [], jnp.full((sub, 1), EMPTY, jnp.float32)
                if block < blocks:
                    begin = block * slots
                    asked = jnp.concatenate(
                        [query[slot, head * KEYS + begin : head * KEYS + begin + slots, :] for head in range(heads)], 0
                    )
                total, summed = 0.0, 0.0
                for at, span in enumerate(spans):
                    if block < blocks:
                        scores = jnp.dot(asked, keys(*span, PADDED), preferred_element_type=jnp.float32)
                        if first and at == 0:
                            scores = jnp.where(key <= time + begin, scores, NEGATIVE)
                        found.append(scores)
                        top = jnp.maximum(top, jnp.max(scores, axis=1, keepdims=True))
                    if held is not None:
                        weights = jnp.exp2(held[0][at] * scale - held[1] * scale)
                        total = total + jnp.sum(weights, axis=1, keepdims=True)
                        summed = summed + lax.dot_general(
                            weights.astype(jnp.bfloat16),
                            keys(*span, 512),
                            (((1,), (1,)), ((), ())),
                            preferred_element_type=jnp.float32,
                        )
                if held is not None:
                    seen = total > 0.0
                    total = jnp.where(seen, total, 1.0)
                    latent = (summed * (1.0 / total)).astype(jnp.bfloat16)
                    level = jnp.where(seen, held[1] * scale + jnp.log2(total), NEGATIVE)
                    level = jnp.broadcast_to(level, (sub, KEYS))
                    high = level.astype(jnp.bfloat16).astype(jnp.float32)
                    middle = (level - high).astype(jnp.bfloat16).astype(jnp.float32)
                    low = level - high - middle
                    third = jnp.where(key == 0, high, jnp.where(key == 1, middle, jnp.where(key == 2, low, 0.0)))
                    third = third.astype(jnp.bfloat16)
                    for head in range(heads):
                        part = slice(head * slots, (head + 1) * slots)
                        place = head * KEYS + (block - 1) * slots
                        latents[slot, place : place + slots, :] = latent[part, :]
                        levels[slot, place : place + slots, :] = third[part, :]
                held = found, top

        @pl.loop(0, 2)
        def _(slot):
            offset = jnp.where(slot == 0, limit_refs[0][0], limit_refs[1][0])
            length = jnp.where(slot == 0, limit_refs[0][1], limit_refs[1][1])
            visible = sum((n * KEYS < offset).astype(jnp.int32) for n in numbers)
            needed = (visible + chunk - 1) // chunk
            used = jnp.where(length > slots, 2, 1)

            if not first:

                @pl.when(needed == 0)
                def _():
                    latents[slot, :, :] = jnp.zeros((rows, 512), jnp.bfloat16)
                    lanes = lax.broadcasted_iota(jnp.int32, (rows, KEYS), 1)
                    levels[slot, :, :] = jnp.where(lanes == 0, NEGATIVE, 0.0).astype(jnp.bfloat16)

            for chunks in range(1 - first, shards // chunk + 1):
                for blocks in (1, 2):

                    @pl.when((needed == chunks) & (used == blocks))
                    def _():
                        work(slot, blocks, chunks)

        copies[-1].wait()
        for head in range(heads):
            part = slice(head * KEYS, (head + 1) * KEYS)
            for slot, ref in enumerate(out_refs):
                values = jnp.dot(latents[slot, part, :], weight[head], preferred_element_type=jnp.float32)
                ref[part, :KEYS] = values.astype(jnp.bfloat16)
                ref[part, KEYS:] = levels[slot, part, :]

    smem, hbm, vmem = (pl.BlockSpec(memory_space=s) for s in (pltpu.SMEM, pl.ANY, pltpu.VMEM))
    total_keys = (shards + first) * KEYS
    made_from = [
        pltpu.VMEM((2, rows, KEYS), jnp.bfloat16),
        pltpu.VMEM((rows, KEYS), jnp.float32),
        pltpu.VMEM((2, heads, 64, KEYS), jnp.bfloat16),
        pltpu.VMEM((heads, KEYS, 512), jnp.bfloat16),
    ]
    return pl.pallas_call(
        kernel,
        in_specs=[smem] * 2 + [hbm] * (len(operands) - 2),
        out_specs=[vmem] * (2 + first),
        out_shape=[jax.ShapeDtypeStruct((rows, 2 * KEYS), jnp.bfloat16)] * 2
        + [jax.ShapeDtypeStruct((2, rows, PADDED), jnp.bfloat16)] * first,
        scratch_shapes=[
            pltpu.VMEM((shards + first, PADDED, KEYS), jnp.bfloat16),
            pltpu.VMEM((heads, 512, KEYS), jnp.bfloat16),
            pltpu.VMEM((2, rows, 512), jnp.bfloat16),
            pltpu.VMEM((2, rows, KEYS), jnp.bfloat16),
            *(made_from if first else [pltpu.VMEM((2, rows, PADDED), jnp.bfloat16)]),
            pltpu.SemaphoreType.DMA((len(operands) + shards,)),
        ],
        compiler_params=pltpu.CompilerParams(vmem_limit_bytes=(57 if first else 40) * 2**20),
        cost_estimate=pl.CostEstimate(
            flops=4 * rows * total_keys * (PADDED + 512), bytes_accessed=8 << 20, transcendentals=2 * rows * total_keys
        ),
    )(*operands)


def project(pieces, output_weight, length):
    rows = pieces[0].shape[0]
    heads = rows // KEYS
    width = output_weight.shape[-1]
    tile = 896

    def kernel(length_ref, *refs):
        piece_refs = refs[: len(pieces)]
        weight_ref, out_ref, values = refs[len(pieces) :]

        @pl.when(pl.program_id(0) == 0)
        def _():
            for head in range(heads):
                part = slice(head * KEYS, (head + 1) * KEYS)
                levels = [level_of(ref[part, KEYS:]) for ref in piece_refs]
                top = functools.reduce(jnp.maximum, levels)
                shares = [jnp.exp2(level - top) for level in levels]
                both = functools.reduce(
                    jnp.add, [ref[part, :KEYS].astype(jnp.float32) * s for ref, s in zip(piece_refs, shares)]
                ) / functools.reduce(jnp.add, shares)
                slot = lax.broadcasted_iota(jnp.int32, (KEYS, KEYS), 0)
                values[:, part] = jnp.where(slot < length_ref[0], both, 0.0).astype(jnp.bfloat16)

        out_ref[...] = jnp.dot(values[...], weight_ref[...], preferred_element_type=jnp.float32).astype(jnp.bfloat16)

    return pl.pallas_call(
        kernel,
        grid_spec=pltpu.PrefetchScalarGridSpec(
            num_scalar_prefetch=1,
            grid=(width // tile,),
            in_specs=[pl.BlockSpec(p.shape, lambda i, *_: (0, 0)) for p in pieces]
            + [pl.BlockSpec((rows, tile), lambda i, *_: (0, i))],
            out_specs=pl.BlockSpec((KEYS, tile), lambda i, *_: (0, i)),
            scratch_shapes=[pltpu.VMEM((KEYS, rows), jnp.bfloat16)],
        ),
        out_shape=jax.ShapeDtypeStruct((KEYS, width), jnp.bfloat16),
        compiler_params=pltpu.CompilerParams(vmem_limit_bytes=24 * 2**20),
        cost_estimate=pl.CostEstimate(flops=2 * KEYS * rows * width, bytes_accessed=2 * rows * width, transcendentals=0),
    )(length, *pieces, output_weight)


def body(
    query_content,
    query_rotary,
    prompt_latent,
    prompt_rotary,
    reply_latent,
    reply_rotary,
    key_weight,
    value_weight,
    output_weight,
    lengths,
    offsets,
):
    mine = Shards(jnp.concatenate([prompt_latent, prompt_rotary], 0)[None], lambda *place: start_of(place))
    chip = mine.joined(mine.taken(other_core))
    near, far = chip.taken(fetch(0)), chip.taken(fetch(1))
    ways = (from_x(1), from_x(-1), from_y)
    groups = [[held] + [held.taken(w) for w in ways] for held in (near, far)]

    partner = pairs_from(other_core)
    limits = jnp.concatenate([offsets, lengths])
    limits = limits, lax.ppermute(limits, AXES, partner)
    content = query_content.reshape(-1, query_content.shape[-1])
    rotary = query_rotary[0]
    queries = [content, lax.ppermute(content, AXES, partner), rotary, lax.ppermute(rotary, AXES, partner), key_weight]
    own = reply_latent[0], reply_rotary[0]

    mine_near, sent_near, query = attend(queries, groups[0], limits, own, value_weight)
    mine_far, sent_far = attend([query], groups[1], limits, None, value_weight)
    pieces = [mine_near, mine_far, *(lax.ppermute(sent, AXES, partner) for sent in (sent_near, sent_far))]
    term = project(pieces, output_weight.reshape(-1, output_weight.shape[-1]), lengths)
    parts = lax.all_to_all(term, "head", 0, 0, tiled=True)
    parts = parts.reshape(8, parts.shape[0] // 8, -1).astype(jnp.float32)
    return jnp.sum(parts, 0).astype(jnp.bfloat16)[:, None, :]


def solution(mesh):
    placed = (
        P("blk", None, "head", None),
        P("blk", "head", None, None),
        P(None, "blk"),
        P(None, "blk"),
        P("blk", None, None),
        P("blk", None, None),
        P("head", None, None),
        P("head", None, None),
        P("head", None, None),
        P("blk"),
        P("blk"),
    )
    return jax.shard_map(
        body, mesh=mesh, in_specs=placed, out_specs=P("head", "blk", None), check_vma=False
    )
```

```python
import functools
import itertools
import math

import jax
import jax.numpy as jnp
from jax import lax
from jax.experimental import pallas as pl
from jax.experimental.pallas import tpu as pltpu
from jax.sharding import PartitionSpec as P

NEGATIVE = -1e30
EMPTY = -1e29
AXES = ("blk", "head")
SIZES = (2, 8, 2, 4, 2)
KEYS = 128
DEPTH = 576
PADDED = 640


def linear(place):
    index = 0
    for value, size in zip(place, SIZES):
        index = index * size + value % size
    return index


PLACES = list(itertools.product(*map(range, SIZES)))


def pairs_from(source):
    return [(linear(source(*place)), linear(place)) for place in PLACES]


def side(core):
    return 1 - 2 * core


def fetch(far):
    def source(yh, z, core, x, yl):
        wide = (x + 2 * yl) % 4 // 2
        distance = (3 + wide * (1 - 4 * core)) if far else 1 + wide
        odd = x % 2
        return (yh + odd) % 2, (z + 8 - distance * side(core)) % 8, core, x, (yl + odd) % 2

    return source


def other_core(yh, z, core, x, yl):
    return yh, z, 1 - core, x, yl


def from_x(step):
    return lambda yh, z, core, x, yl: (yh, z, core, (x + 4 - step) % 4, yl)


def from_y(yh, z, core, x, yl):
    return yh, z, core, x, 1 - yl


def start_of(place):
    yh, z, core, _, _ = place
    return [(yh * 8 + z) * 2 + core]


class Shards:
    def __init__(self, array, numbers):
        self.array, self.numbers, self.count = array, numbers, array.shape[0]

    def taken(self, source):
        numbers = self.numbers
        return Shards(lax.ppermute(self.array, AXES, pairs_from(source)), lambda *place: numbers(*source(*place)))

    def joined(self, other):
        a, b = self.numbers, other.numbers
        return Shards(jnp.concatenate([self.array, other.array], 0), lambda *place: a(*place) + b(*place))


def own_place():
    blk, head = lax.axis_index("blk"), lax.axis_index("head")
    return blk // 16, blk // 2 % 8, blk % 2, head // 2, head % 2


def spread():
    return (lax.broadcasted_iota(jnp.int32, (KEYS, KEYS), 0) < 3).astype(jnp.float32).astype(jnp.bfloat16)


def level_of(parts):
    return jnp.dot(parts, spread(), preferred_element_type=jnp.float32)


def in_thirds(level):
    lane = lax.broadcasted_iota(jnp.int32, level.shape, 1)
    high = level.astype(jnp.bfloat16).astype(jnp.float32)
    middle = (level - high).astype(jnp.bfloat16).astype(jnp.float32)
    low = level - high - middle
    parts = jnp.where(lane == 0, high, jnp.where(lane == 1, middle, jnp.where(lane == 2, low, 0.0)))
    return parts.astype(jnp.bfloat16)


def attend(queries, group, limits, own, before, value_weight):
    heads = value_weight.shape[0]
    rows = heads * KEYS
    shards = sum(g.count for g in group)
    first = int(own is not None)
    chunk = 4
    slots = 64
    sub = heads * slots
    scale = (128 + 64) ** -0.5 * math.log2(math.e)
    operands = [*limits, *queries, value_weight, *(g.array for g in group), *(own or before)]

    def kernel(*refs):
        refs = list(refs)
        limit_refs = [refs.pop(0) for _ in range(2)]
        query_refs = [refs.pop(0) for _ in queries]
        weight_ref = refs.pop(0)
        group_refs = [refs.pop(0) for _ in group]
        own_refs = [refs.pop(0) for _ in range(2)]
        out_refs = [refs.pop(0) for _ in range(2)]
        if first:
            query, table, weight, latents, levels, content, wide, rotary, absorbed, sems = refs
        else:
            table, weight, latents, levels, query, earlier, sems = refs
        copies = []

        def copy(start, end):
            made = pltpu.make_async_copy(start, end, sems.at[len(copies)])
            made.start()
            copies.append(made)

        place = own_place()
        numbers = [n for g in group for n in g.numbers(*place)]
        ranks = [sum((other < n).astype(jnp.int32) for other in numbers if other is not n) for n in numbers]
        if first:
            for ref, end in zip(query_refs, (content.at[0], content.at[1], rotary.at[0], rotary.at[1], absorbed)):
                copy(ref, end)
        else:
            copy(query_refs[0], query)
        for i, rank in enumerate(ranks):
            copy(group_refs[i // 2].at[i % 2], table.at[first + rank, pl.ds(0, DEPTH), :])
        if first:
            copy(own_refs[0], table.at[0, pl.ds(0, 512), :])
            copy(own_refs[1], table.at[0, pl.ds(512, 64), :])
        else:
            copy(own_refs[0], earlier.at[0])
            copy(own_refs[1], earlier.at[1])
        copy(weight_ref, weight)

        row = lax.broadcasted_iota(jnp.int32, (16, KEYS), 0)
        lane = lax.broadcasted_iota(jnp.int32, (16, KEYS), 1)
        limit = jnp.where(row == 0, limit_refs[0][0], limit_refs[1][0])
        hide = [(0, row == 1)] if first else []
        hide += [(first + rank, (row < 2) & (n * KEYS + lane >= limit)) for n, rank in zip(numbers, ranks)]
        for at, hidden in hide:
            table[at, DEPTH : DEPTH + 16, :] = jnp.where(hidden, NEGATIVE, 0.0).astype(jnp.bfloat16)
            table[at, DEPTH + 16 : PADDED, :] = jnp.zeros((PADDED - DEPTH - 16, KEYS), jnp.bfloat16)
        for made in copies[: len(queries)]:
            made.wait()
        if first:
            lanes = lax.broadcasted_iota(jnp.int32, (KEYS, PADDED - DEPTH), 1)
            for slot in range(2):
                wide[...] = content[slot].astype(jnp.float32)
                for head in range(heads):
                    part = slice(head * KEYS, (head + 1) * KEYS)
                    asked = wide[pl.ds(head, KEYS, stride=heads), :].astype(jnp.bfloat16)
                    latent = jnp.dot(asked, absorbed[head], preferred_element_type=jnp.float32)
                    query[slot, part, 0:512] = latent.astype(jnp.bfloat16)
                    rest = [rotary[slot, head].astype(jnp.float32).T, (lanes == slot).astype(jnp.float32)]
                    query[slot, part, 512:PADDED] = jnp.concatenate(rest, 1).astype(jnp.bfloat16)
        late = 1 if first else 3
        for made in copies[len(queries) : -late]:
            made.wait()

        def keys(begin, count, depth):
            return jnp.concatenate([table[at, :depth, :] for at in range(begin, begin + count)], 1)

        def work(slot, blocks, chunks):
            spans = [(0, 1)] * first + [(first + i * chunk, chunk) for i in range(chunks)]
            key = lax.broadcasted_iota(jnp.int32, (sub, KEYS), 1)
            time = lax.broadcasted_iota(jnp.int32, (sub, KEYS), 0) % slots
            held = None
            for block in range(blocks + 1):
                found, top = [], jnp.full((sub, 1), EMPTY, jnp.float32)
                if block < blocks:
                    begin = block * slots
                    asked = jnp.concatenate(
                        [query[slot, head * KEYS + begin : head * KEYS + begin + slots, :] for head in range(heads)], 0
                    )
                total, summed = 0.0, 0.0
                for at, span in enumerate(spans):
                    if block < blocks:
                        scores = jnp.dot(asked, keys(*span, PADDED), preferred_element_type=jnp.float32)
                        if first and at == 0:
                            scores = jnp.where(key <= time + begin, scores, NEGATIVE)
                        found.append(scores)
                        top = jnp.maximum(top, jnp.max(scores, axis=1, keepdims=True))
                    if held is not None:
                        weights = jnp.exp2(held[0][at] * scale - held[1] * scale)
                        total = total + jnp.sum(weights, axis=1, keepdims=True)
                        summed = summed + lax.dot_general(
                            weights.astype(jnp.bfloat16),
                            keys(*span, 512),
                            (((1,), (1,)), ((), ())),
                            preferred_element_type=jnp.float32,
                        )
                if held is not None:
                    seen = total > 0.0
                    total = jnp.where(seen, total, 1.0)
                    latent = (summed * (1.0 / total)).astype(jnp.bfloat16)
                    level = jnp.where(seen, held[1] * scale + jnp.log2(total), NEGATIVE)
                    level = jnp.broadcast_to(level, (sub, KEYS))
                    third = in_thirds(level)
                    for head in range(heads):
                        part = slice(head * slots, (head + 1) * slots)
                        place = head * KEYS + (block - 1) * slots
                        latents[slot, place : place + slots, :] = latent[part, :]
                        levels[slot, place : place + slots, :] = third[part, :]
                held = found, top

        @pl.loop(0, 2)
        def _(slot):
            offset = jnp.where(slot == 0, limit_refs[0][0], limit_refs[1][0])
            length = jnp.where(slot == 0, limit_refs[0][1], limit_refs[1][1])
            visible = sum((n * KEYS < offset).astype(jnp.int32) for n in numbers)
            needed = (visible + chunk - 1) // chunk
            used = jnp.where(length > slots, 2, 1)

            if not first:

                @pl.when(needed == 0)
                def _():
                    latents[slot, :, :] = jnp.zeros((rows, 512), jnp.bfloat16)
                    lanes = lax.broadcasted_iota(jnp.int32, (rows, KEYS), 1)
                    levels[slot, :, :] = jnp.where(lanes == 0, NEGATIVE, 0.0).astype(jnp.bfloat16)

            for chunks in range(1 - first, shards // chunk + 1):
                for blocks in (1, 2):

                    @pl.when((needed == chunks) & (used == blocks))
                    def _():
                        work(slot, blocks, chunks)

        for made in copies[-late:]:
            made.wait()
        for head in range(heads):
            part = slice(head * KEYS, (head + 1) * KEYS)
            both = jnp.concatenate([latents[slot, part, :] for slot in range(2)], 0)
            both = jnp.dot(both, weight[head], preferred_element_type=jnp.float32)
            for slot, ref in enumerate(out_refs):
                values = both[slot * KEYS : (slot + 1) * KEYS, :]
                if first:
                    ref[part, :KEYS] = values.astype(jnp.bfloat16)
                    ref[part, KEYS:] = levels[slot, part, :]
                    continue
                one, two = level_of(earlier[slot, part, KEYS:]), level_of(levels[slot, part, :])
                top = jnp.maximum(one, two)
                a, b = jnp.exp2(one - top), jnp.exp2(two - top)
                values = (earlier[slot, part, :KEYS].astype(jnp.float32) * a + values * b) / (a + b)
                ref[part, :KEYS] = values.astype(jnp.bfloat16)
                ref[part, KEYS:] = in_thirds(top + jnp.log2(a + b))

    smem, hbm, vmem = (pl.BlockSpec(memory_space=s) for s in (pltpu.SMEM, pl.ANY, pltpu.VMEM))
    total_keys = (shards + first) * KEYS
    made_from = [
        pltpu.VMEM((2, rows, KEYS), jnp.bfloat16),
        pltpu.VMEM((rows, KEYS), jnp.float32),
        pltpu.VMEM((2, heads, 64, KEYS), jnp.bfloat16),
        pltpu.VMEM((heads, KEYS, 512), jnp.bfloat16),
    ]
    return pl.pallas_call(
        kernel,
        in_specs=[smem] * 2 + [hbm] * (len(operands) - 2),
        out_specs=[vmem] * (2 + first),
        out_shape=[jax.ShapeDtypeStruct((rows, 2 * KEYS), jnp.bfloat16)] * 2
        + [jax.ShapeDtypeStruct((2, rows, PADDED), jnp.bfloat16)] * first,
        scratch_shapes=[
            pltpu.VMEM((shards + first, PADDED, KEYS), jnp.bfloat16),
            pltpu.VMEM((heads, 512, KEYS), jnp.bfloat16),
            pltpu.VMEM((2, rows, 512), jnp.bfloat16),
            pltpu.VMEM((2, rows, KEYS), jnp.bfloat16),
            *(made_from if first else [pltpu.VMEM((2, rows, PADDED), jnp.bfloat16), pltpu.VMEM((2, rows, 2 * KEYS), jnp.bfloat16)]),
            pltpu.SemaphoreType.DMA((len(operands) + shards,)),
        ],
        compiler_params=pltpu.CompilerParams(vmem_limit_bytes=(57 if first else 52) * 2**20),
        cost_estimate=pl.CostEstimate(
            flops=4 * rows * total_keys * (PADDED + 512), bytes_accessed=8 << 20, transcendentals=2 * rows * total_keys
        ),
    )(*operands)


def project(pieces, output_weight, length):
    rows = pieces[0].shape[0]
    heads = rows // KEYS
    width = output_weight.shape[-1]
    tile = 896

    def kernel(length_ref, *refs):
        piece_refs = refs[: len(pieces)]
        weight_ref, out_ref, values = refs[len(pieces) :]

        @pl.when(pl.program_id(0) == 0)
        def _():
            for head in range(heads):
                part = slice(head * KEYS, (head + 1) * KEYS)
                levels = [level_of(ref[part, KEYS:]) for ref in piece_refs]
                top = functools.reduce(jnp.maximum, levels)
                shares = [jnp.exp2(level - top) for level in levels]
                both = functools.reduce(
                    jnp.add, [ref[part, :KEYS].astype(jnp.float32) * s for ref, s in zip(piece_refs, shares)]
                ) / functools.reduce(jnp.add, shares)
                slot = lax.broadcasted_iota(jnp.int32, (KEYS, KEYS), 0)
                values[:, part] = jnp.where(slot < length_ref[0], both, 0.0).astype(jnp.bfloat16)

        out_ref[...] = jnp.dot(values[...], weight_ref[...], preferred_element_type=jnp.float32).astype(jnp.bfloat16)

    return pl.pallas_call(
        kernel,
        grid_spec=pltpu.PrefetchScalarGridSpec(
            num_scalar_prefetch=1,
            grid=(width // tile,),
            in_specs=[pl.BlockSpec(p.shape, lambda i, *_: (0, 0)) for p in pieces]
            + [pl.BlockSpec((rows, tile), lambda i, *_: (0, i))],
            out_specs=pl.BlockSpec((KEYS, tile), lambda i, *_: (0, i)),
            scratch_shapes=[pltpu.VMEM((KEYS, rows), jnp.bfloat16)],
        ),
        out_shape=jax.ShapeDtypeStruct((KEYS, width), jnp.bfloat16),
        compiler_params=pltpu.CompilerParams(vmem_limit_bytes=24 * 2**20),
        cost_estimate=pl.CostEstimate(flops=2 * KEYS * rows * width, bytes_accessed=2 * rows * width, transcendentals=0),
    )(length, *pieces, output_weight)


def body(
    query_content,
    query_rotary,
    prompt_latent,
    prompt_rotary,
    reply_latent,
    reply_rotary,
    key_weight,
    value_weight,
    output_weight,
    lengths,
    offsets,
):
    mine = Shards(jnp.concatenate([prompt_latent, prompt_rotary], 0)[None], lambda *place: start_of(place))
    chip = mine.joined(mine.taken(other_core))
    near, far = chip.taken(fetch(0)), chip.taken(fetch(1))
    ways = (from_x(1), from_x(-1), from_y)
    groups = [[held] + [held.taken(w) for w in ways] for held in (near, far)]

    partner = pairs_from(other_core)
    limits = jnp.concatenate([offsets, lengths])
    limits = limits, lax.ppermute(limits, AXES, partner)
    content = query_content.reshape(-1, query_content.shape[-1])
    rotary = query_rotary[0]
    queries = [content, lax.ppermute(content, AXES, partner), rotary, lax.ppermute(rotary, AXES, partner), key_weight]
    own = reply_latent[0], reply_rotary[0]

    *pieces, query = attend(queries, groups[0], limits, own, None, value_weight)
    mine_part, sent = attend([query], groups[1], limits, None, pieces, value_weight)
    pieces = mine_part, lax.ppermute(sent, AXES, partner)
    term = project(pieces, output_weight.reshape(-1, output_weight.shape[-1]), lengths)
    parts = lax.all_to_all(term, "head", 0, 0, tiled=True)
    parts = parts.reshape(8, parts.shape[0] // 8, -1).astype(jnp.float32)
    return jnp.sum(parts, 0).astype(jnp.bfloat16)[:, None, :]


def solution(mesh):
    placed = (
        P("blk", None, "head", None),
        P("blk", "head", None, None),
        P(None, "blk"),
        P(None, "blk"),
        P("blk", None, None),
        P("blk", None, None),
        P("head", None, None),
        P("head", None, None),
        P("head", None, None),
        P("blk"),
        P("blk"),
    )
    return jax.shard_map(
        body, mesh=mesh, in_specs=placed, out_specs=P("head", "blk", None), check_vma=False
    )
```

```python
import functools
import itertools
import math

import jax
import jax.numpy as jnp
from jax import lax
from jax.experimental import pallas as pl
from jax.experimental.pallas import tpu as pltpu
from jax.sharding import PartitionSpec as P

NEGATIVE = -1e30
EMPTY = -1e29
AXES = ("blk", "head")
SIZES = (2, 8, 2, 4, 2)
KEYS = 128
DEPTH = 576
PADDED = 640


def linear(place):
    index = 0
    for value, size in zip(place, SIZES):
        index = index * size + value % size
    return index


PLACES = list(itertools.product(*map(range, SIZES)))


def pairs_from(source):
    return [(linear(source(*place)), linear(place)) for place in PLACES]


def side(core):
    return 1 - 2 * core


def fetch(far):
    def source(yh, z, core, x, yl):
        wide = (x + 2 * yl) % 4 // 2
        distance = (3 + wide * (1 - 4 * core)) if far else 1 + wide
        odd = x % 2
        return (yh + odd) % 2, (z + 8 - distance * side(core)) % 8, core, x, (yl + odd) % 2

    return source


def other_core(yh, z, core, x, yl):
    return yh, z, 1 - core, x, yl


def from_x(step):
    return lambda yh, z, core, x, yl: (yh, z, core, (x + 4 - step) % 4, yl)


def from_y(yh, z, core, x, yl):
    return yh, z, core, x, 1 - yl


def start_of(place):
    yh, z, core, _, _ = place
    return [(yh * 8 + z) * 2 + core]


class Shards:
    def __init__(self, array, numbers):
        self.array, self.numbers, self.count = array, numbers, array.shape[0]

    def taken(self, source):
        numbers = self.numbers
        return Shards(lax.ppermute(self.array, AXES, pairs_from(source)), lambda *place: numbers(*source(*place)))

    def joined(self, other):
        a, b = self.numbers, other.numbers
        return Shards(jnp.concatenate([self.array, other.array], 0), lambda *place: a(*place) + b(*place))


def own_place():
    blk, head = lax.axis_index("blk"), lax.axis_index("head")
    return blk // 16, blk // 2 % 8, blk % 2, head // 2, head % 2


def spread():
    return (lax.broadcasted_iota(jnp.int32, (KEYS, KEYS), 0) < 3).astype(jnp.float32).astype(jnp.bfloat16)


def level_of(parts):
    return jnp.dot(parts, spread(), preferred_element_type=jnp.float32)


def in_thirds(level):
    lane = lax.broadcasted_iota(jnp.int32, level.shape, 1)
    high = level.astype(jnp.bfloat16).astype(jnp.float32)
    middle = (level - high).astype(jnp.bfloat16).astype(jnp.float32)
    low = level - high - middle
    parts = jnp.where(lane == 0, high, jnp.where(lane == 1, middle, jnp.where(lane == 2, low, 0.0)))
    return parts.astype(jnp.bfloat16)


def attend(queries, group, limits, own, before, value_weight):
    heads = value_weight.shape[0]
    rows = heads * KEYS
    shards = sum(g.count for g in group)
    first = int(own is not None)
    chunk = 4
    slots = 64
    sub = heads * slots
    scale = (128 + 64) ** -0.5 * math.log2(math.e)
    operands = [*limits, *queries, value_weight, *(g.array for g in group), *(own or before)]

    def kernel(*refs):
        refs = list(refs)
        limit_refs = [refs.pop(0) for _ in range(2)]
        query_refs = [refs.pop(0) for _ in queries]
        weight_ref = refs.pop(0)
        group_refs = [refs.pop(0) for _ in group]
        own_refs = [refs.pop(0) for _ in range(2)]
        out_refs = [refs.pop(0) for _ in range(2)]
        if first:
            query, table, weight, latents, levels, content, wide, rotary, absorbed, sems = refs
        else:
            table, weight, latents, levels, query, earlier, sems = refs
        copies = []

        def copy(start, end):
            made = pltpu.make_async_copy(start, end, sems.at[len(copies)])
            made.start()
            copies.append(made)

        place = own_place()
        numbers = [n for g in group for n in g.numbers(*place)]
        ranks = [sum((other < n).astype(jnp.int32) for other in numbers if other is not n) for n in numbers]
        if first:
            for ref, end in zip(query_refs, (content.at[0], content.at[1], rotary.at[0], rotary.at[1], absorbed)):
                copy(ref, end)
        else:
            copy(query_refs[0], query)
        for i, rank in enumerate(ranks):
            copy(group_refs[i // 2].at[i % 2], table.at[first + rank, pl.ds(0, DEPTH), :])
        if first:
            copy(own_refs[0], table.at[0, pl.ds(0, 512), :])
            copy(own_refs[1], table.at[0, pl.ds(512, 64), :])
        else:
            copy(own_refs[0], earlier.at[0])
            copy(own_refs[1], earlier.at[1])
        copy(weight_ref, weight)

        row = lax.broadcasted_iota(jnp.int32, (16, KEYS), 0)
        lane = lax.broadcasted_iota(jnp.int32, (16, KEYS), 1)
        limit = jnp.where(row == 0, limit_refs[0][0], limit_refs[1][0])
        hide = [(0, row == 1)] if first else []
        hide += [(first + rank, (row < 2) & (n * KEYS + lane >= limit)) for n, rank in zip(numbers, ranks)]
        for at, hidden in hide:
            table[at, DEPTH : DEPTH + 16, :] = jnp.where(hidden, NEGATIVE, 0.0).astype(jnp.bfloat16)
            table[at, DEPTH + 16 : PADDED, :] = jnp.zeros((PADDED - DEPTH - 16, KEYS), jnp.bfloat16)
        for made in copies[: len(queries)]:
            made.wait()
        if first:
            lanes = lax.broadcasted_iota(jnp.int32, (KEYS, PADDED - DEPTH), 1)
            for slot in range(2):
                wide[...] = content[slot].astype(jnp.float32)
                for head in range(heads):
                    part = slice(head * KEYS, (head + 1) * KEYS)
                    asked = wide[pl.ds(head, KEYS, stride=heads), :].astype(jnp.bfloat16)
                    latent = jnp.dot(asked, absorbed[head], preferred_element_type=jnp.float32)
                    query[slot, part, 0:512] = latent.astype(jnp.bfloat16)
                    rest = [rotary[slot, head].astype(jnp.float32).T, (lanes == slot).astype(jnp.float32)]
                    query[slot, part, 512:PADDED] = jnp.concatenate(rest, 1).astype(jnp.bfloat16)
        late = 1 if first else 3
        for made in copies[len(queries) : -late]:
            made.wait()

        def keys(begin, count, depth):
            return jnp.concatenate([table[at, :depth, :] for at in range(begin, begin + count)], 1)

        def work(slot, blocks, chunks):
            spans = [(0, 1)] * first + [(first + i * chunk, chunk) for i in range(chunks)]
            key = lax.broadcasted_iota(jnp.int32, (sub, KEYS), 1)
            time = lax.broadcasted_iota(jnp.int32, (sub, KEYS), 0) % slots
            held = None
            for block in range(blocks + 1):
                found, top = [], jnp.full((sub, 1), EMPTY, jnp.float32)
                if block < blocks:
                    begin = block * slots
                    asked = jnp.concatenate(
                        [query[slot, head * KEYS + begin : head * KEYS + begin + slots, :] for head in range(heads)], 0
                    )
                total, summed = 0.0, 0.0
                for at, span in enumerate(spans):
                    if block < blocks:
                        scores = jnp.dot(asked, keys(*span, PADDED), preferred_element_type=jnp.float32)
                        if first and at == 0:
                            scores = jnp.where(key <= time + begin, scores, NEGATIVE)
                        found.append(scores)
                        top = jnp.maximum(top, jnp.max(scores, axis=1, keepdims=True))
                    if held is not None:
                        weights = jnp.exp2(held[0][at] * scale - held[1] * scale)
                        total = total + jnp.sum(weights, axis=1, keepdims=True)
                        summed = summed + lax.dot_general(
                            weights.astype(jnp.bfloat16),
                            keys(*span, 512),
                            (((1,), (1,)), ((), ())),
                            preferred_element_type=jnp.float32,
                        )
                if held is not None:
                    seen = total > 0.0
                    total = jnp.where(seen, total, 1.0)
                    latent = (summed * (1.0 / total)).astype(jnp.bfloat16)
                    level = jnp.where(seen, held[1] * scale + jnp.log2(total), NEGATIVE)
                    level = jnp.broadcast_to(level, (sub, KEYS))
                    third = in_thirds(level)
                    for head in range(heads):
                        part = slice(head * slots, (head + 1) * slots)
                        place = head * KEYS + (block - 1) * slots
                        latents[slot, place : place + slots, :] = latent[part, :]
                        levels[slot, place : place + slots, :] = third[part, :]
                held = found, top

        @pl.loop(0, 2)
        def _(slot):
            offset = jnp.where(slot == 0, limit_refs[0][0], limit_refs[1][0])
            length = jnp.where(slot == 0, limit_refs[0][1], limit_refs[1][1])
            visible = sum((n * KEYS < offset).astype(jnp.int32) for n in numbers)
            needed = (visible + chunk - 1) // chunk
            used = jnp.where(length > slots, 2, 1)

            if not first:

                @pl.when(needed == 0)
                def _():
                    latents[slot, :, :] = jnp.zeros((rows, 512), jnp.bfloat16)
                    lanes = lax.broadcasted_iota(jnp.int32, (rows, KEYS), 1)
                    levels[slot, :, :] = jnp.where(lanes == 0, NEGATIVE, 0.0).astype(jnp.bfloat16)

            for chunks in range(1 - first, shards // chunk + 1):
                for blocks in (1, 2):

                    @pl.when((needed == chunks) & (used == blocks))
                    def _():
                        work(slot, blocks, chunks)

        for made in copies[-late:]:
            made.wait()
        for head in range(heads):
            part = slice(head * KEYS, (head + 1) * KEYS)
            both = jnp.concatenate([latents[slot, part, :] for slot in range(2)], 0)
            both = jnp.dot(both, weight[head], preferred_element_type=jnp.float32)
            for slot, ref in enumerate(out_refs):
                values = both[slot * KEYS : (slot + 1) * KEYS, :]
                if first:
                    ref[part, :KEYS] = values.astype(jnp.bfloat16)
                    ref[part, KEYS:] = levels[slot, part, :]
                    continue
                one, two = level_of(earlier[slot, part, KEYS:]), level_of(levels[slot, part, :])
                top = jnp.maximum(one, two)
                a, b = jnp.exp2(one - top), jnp.exp2(two - top)
                values = (earlier[slot, part, :KEYS].astype(jnp.float32) * a + values * b) / (a + b)
                ref[part, :KEYS] = values.astype(jnp.bfloat16)
                ref[part, KEYS:] = in_thirds(top + jnp.log2(a + b))

    smem, hbm, vmem = (pl.BlockSpec(memory_space=s) for s in (pltpu.SMEM, pl.ANY, pltpu.VMEM))
    total_keys = (shards + first) * KEYS
    made_from = [
        pltpu.VMEM((2, rows, KEYS), jnp.bfloat16),
        pltpu.VMEM((rows, KEYS), jnp.float32),
        pltpu.VMEM((2, heads, 64, KEYS), jnp.bfloat16),
        pltpu.VMEM((heads, KEYS, 512), jnp.bfloat16),
    ]
    return pl.pallas_call(
        kernel,
        in_specs=[smem] * 2 + [hbm] * (len(operands) - 2),
        out_specs=[vmem] * (2 + first),
        out_shape=[jax.ShapeDtypeStruct((rows, 2 * KEYS), jnp.bfloat16)] * 2
        + [jax.ShapeDtypeStruct((2, rows, PADDED), jnp.bfloat16)] * first,
        scratch_shapes=[
            pltpu.VMEM((shards + first, PADDED, KEYS), jnp.bfloat16),
            pltpu.VMEM((heads, 512, KEYS), jnp.bfloat16),
            pltpu.VMEM((2, rows, 512), jnp.bfloat16),
            pltpu.VMEM((2, rows, KEYS), jnp.bfloat16),
            *(made_from if first else [pltpu.VMEM((2, rows, PADDED), jnp.bfloat16), pltpu.VMEM((2, rows, 2 * KEYS), jnp.bfloat16)]),
            pltpu.SemaphoreType.DMA((len(operands) + shards,)),
        ],
        compiler_params=pltpu.CompilerParams(vmem_limit_bytes=(57 if first else 52) * 2**20),
        cost_estimate=pl.CostEstimate(
            flops=4 * rows * total_keys * (PADDED + 512), bytes_accessed=8 << 20, transcendentals=2 * rows * total_keys
        ),
    )(*operands)


def project(pieces, output_weight, length):
    rows = pieces[0].shape[0]
    heads = rows // KEYS
    width = output_weight.shape[-1]
    tile = 896

    def kernel(length_ref, *refs):
        piece_refs = refs[: len(pieces)]
        weight_ref, out_ref, values = refs[len(pieces) :]
        for head in range(heads):
            part = slice(head * KEYS, (head + 1) * KEYS)
            levels = [level_of(ref[part, KEYS:]) for ref in piece_refs]
            top = functools.reduce(jnp.maximum, levels)
            shares = [jnp.exp2(level - top) for level in levels]
            both = functools.reduce(
                jnp.add, [ref[part, :KEYS].astype(jnp.float32) * s for ref, s in zip(piece_refs, shares)]
            ) / functools.reduce(jnp.add, shares)
            slot = lax.broadcasted_iota(jnp.int32, (KEYS, KEYS), 0)
            values[:, part] = jnp.where(slot < length_ref[0], both, 0.0).astype(jnp.bfloat16)

        for begin in range(0, width, tile):
            part = slice(begin, begin + tile)
            found = jnp.dot(values[...], weight_ref[:, part], preferred_element_type=jnp.float32)
            out_ref[:, part] = found.astype(jnp.bfloat16)

    vmem = pl.BlockSpec(memory_space=pltpu.VMEM)
    return pl.pallas_call(
        kernel,
        in_specs=[pl.BlockSpec(memory_space=pltpu.SMEM)] + [vmem] * (len(pieces) + 1),
        out_specs=vmem,
        out_shape=jax.ShapeDtypeStruct((KEYS, width), jnp.bfloat16),
        scratch_shapes=[pltpu.VMEM((KEYS, rows), jnp.bfloat16)],
        compiler_params=pltpu.CompilerParams(vmem_limit_bytes=24 * 2**20),
        cost_estimate=pl.CostEstimate(flops=2 * KEYS * rows * width, bytes_accessed=2 * rows * width, transcendentals=0),
    )(length, *pieces, output_weight)


def body(
    query_content,
    query_rotary,
    prompt_latent,
    prompt_rotary,
    reply_latent,
    reply_rotary,
    key_weight,
    value_weight,
    output_weight,
    lengths,
    offsets,
):
    mine = Shards(jnp.concatenate([prompt_latent, prompt_rotary], 0)[None], lambda *place: start_of(place))
    chip = mine.joined(mine.taken(other_core))
    near, far = chip.taken(fetch(0)), chip.taken(fetch(1))
    ways = (from_x(1), from_x(-1), from_y)
    groups = [[held] + [held.taken(w) for w in ways] for held in (near, far)]

    partner = pairs_from(other_core)
    limits = jnp.concatenate([offsets, lengths])
    limits = limits, lax.ppermute(limits, AXES, partner)
    content = query_content.reshape(-1, query_content.shape[-1])
    rotary = query_rotary[0]
    queries = [content, lax.ppermute(content, AXES, partner), rotary, lax.ppermute(rotary, AXES, partner), key_weight]
    own = reply_latent[0], reply_rotary[0]

    *pieces, query = attend(queries, groups[0], limits, own, None, value_weight)
    mine_part, sent = attend([query], groups[1], limits, None, pieces, value_weight)
    pieces = mine_part, lax.ppermute(sent, AXES, partner)
    term = project(pieces, output_weight.reshape(-1, output_weight.shape[-1]), lengths)
    parts = lax.all_to_all(term, "head", 0, 0, tiled=True)
    parts = parts.reshape(8, parts.shape[0] // 8, -1).astype(jnp.float32)
    return jnp.sum(parts, 0).astype(jnp.bfloat16)[:, None, :]


def solution(mesh):
    placed = (
        P("blk", None, "head", None),
        P("blk", "head", None, None),
        P(None, "blk"),
        P(None, "blk"),
        P("blk", None, None),
        P("blk", None, None),
        P("head", None, None),
        P("head", None, None),
        P("head", None, None),
        P("blk"),
        P("blk"),
    )
    return jax.shard_map(
        body, mesh=mesh, in_specs=placed, out_specs=P("head", "blk", None), check_vma=False
    )
```
